32 devices in a mesh: tgt: 4 (over x, core), src: 8 (over z, y).
Axes of the slice: x: 2, y: 2, z: 4, core: 2. Of those that a mesh axis runs over, the one named last changes fastest.
Arguments:
- multipoles: float32 [512, 16, 128], P(('src', 'tgt')), may hold values from -6 to 6
- couplings: float32 [64, 288, 128, 128], P('tgt', 'src'), may hold values from -0.0390625 to 0.0390625
- slot_sources: int32 [64, 288], P('tgt', 'src'), may hold values from -1 to 511, as said below
Outputs:
- local_coeffs: float32 [1024, 128], P(('tgt', 'src'))
The draws below stay inside these ranges and needn't reach their ends.
Inputs may be any that keep to these rules, and one draw needn't show every extreme that they name: `slot_sources`: columns j * 36 to (j + 1) * 36 - 1 of a row name only clusters of source block j, ids j * 16 * 4 to (j + 1) * 16 * 4 - 1, or -1. Each row names exactly 189 distinct clusters; in every row one block's 36 slots are all used.
All inputs are finite; a program needn't handle non-finite values.
Results may differ from the reference program's by a relative error of at most 0.0003.
Values sent between devices are 32-bit elements; how exact they have to be, the bound alone decides.
A program may use at most 128 MiB of HBM per device.

```python
import jax
import jax.numpy as jnp
from jax import lax

RANK = 128
NRHS = 16
PARTNERS = 189
CL_DEV = 16
SLOTS = 36
TARGETS = 64
CLUSTERS = 512
N_TGT = 4
N_SRC = 8


def draw_slot_sources(key, part):
    key = jax.random.fold_in(key, 11)
    key_home, key_order, key_pick = jax.random.split(key, 3)
    blocks = N_SRC
    block_size = CL_DEV * N_TGT
    home = jax.random.randint(key_home, (TARGETS,), 0, blocks)
    orders = jax.vmap(lambda k: jax.random.permutation(k, blocks))(jax.random.split(key_order, TARGETS))
    position = jnp.argsort(orders, axis=1, stable=True)
    remain = PARTNERS - SLOTS
    base_count = remain // (blocks - 1)
    extra = remain - base_count * (blocks - 1)
    home_position = jnp.take_along_axis(position, home[:, None], axis=1)
    limit = extra + (home_position < extra).astype(jnp.int32)
    counts = base_count + (position < limit).astype(jnp.int32)
    is_home = jnp.arange(blocks)[None, :] == home[:, None]
    counts = jnp.where(is_home, SLOTS, counts)
    picks = jax.vmap(lambda k: jax.random.permutation(k, block_size))(jax.random.split(key_pick, TARGETS * blocks))
    picks = picks[:, :SLOTS].reshape(TARGETS, blocks, SLOTS)
    ids = jnp.arange(blocks)[None, :, None] * block_size + picks
    ids = jnp.where(jnp.arange(SLOTS)[None, None, :] < counts[:, :, None], ids, -1)
    return ids.reshape(TARGETS, blocks * SLOTS).astype(jnp.int32)


def steps_of(rng, shape, cuts, least, high):
    level = 1.0
    for dim, shards_of in cuts:
        steps = jax.random.uniform(jax.random.fold_in(jax.random.fold_in(rng, 6), dim), (shards_of,), jnp.float32, least / len(cuts), high / len(cuts))
        level = level * jnp.repeat(jnp.exp(steps), shape[dim] // shards_of).reshape((-1,) + (1,) * (len(shape) - 1 - dim))
    return level


def scatter_about(rng, shape, deviation, most, pieces=(), kind=jnp.bfloat16):
    values = jax.random.normal(rng, shape, jnp.float32) * deviation
    if len(pieces) > 0:
        values = steps_of(rng, shape, pieces, -0.22, 0.18) * values
    return jnp.clip(values, min=-most, max=most).astype(kind)


def setup_inputs(seed: int = 0) -> dict:
    key_of = jax.random.split(jax.random.key(seed), 4)
    return {
        "multipoles": scatter_about(key_of[0], (CLUSTERS, NRHS, RANK), 1.0, 6.0, ((0, 32),), jnp.float32),
        "couplings": scatter_about(key_of[1], (TARGETS, N_SRC * SLOTS, RANK, RANK), (RANK * PARTNERS) ** -0.5, 0.0390625, ((0, 4), (1, 8)), jnp.float32),
        "slot_sources": draw_slot_sources(jax.random.fold_in(key_of[3], 71), 0),
    }


def reference(multipoles, couplings, slot_sources):
    def one_target(pair):
        ids, coupling = pair
        live = ids >= 0
        panels = multipoles[jnp.where(live, ids, 0).astype(jnp.int32)]
        panels = jnp.where(live[:, None, None], panels, jnp.zeros_like(panels))
        return jnp.einsum("snr,srq->nq", panels, coupling, precision=lax.Precision.HIGHEST)

    local = lax.map(one_target, (slot_sources, couplings))
    return local.reshape(TARGETS * NRHS, RANK)
```

```python
import functools

import jax
import jax.numpy as jnp
from jax import lax
from jax.experimental import pallas as pl
from jax.experimental.pallas import tpu as pltpu
from jax.sharding import PartitionSpec as P

MESH = pl.DeviceIdType.MESH
DEPTH = 4


def split(value):
    high = value.astype(jnp.bfloat16)
    low = (value - high.astype(jnp.float32)).astype(jnp.bfloat16)
    return high, low


def kernel(n_tgt, n_src, mult_ref, coup_ref, slot_ref, out_ref, held, gathered, panels, partial, received,
           held_sem, own_sem, gather_send, gather_recv, pass_send, pass_recv, part_send, part_recv):
    targets, slots, rank = held.shape[:3]
    clusters, nrhs = mult_ref.shape[:2]
    block = n_tgt * clusters
    rows = out_ref.shape[0]
    steps = min(n_src, targets)
    per_step = targets // steps
    owners = n_src // steps
    chips = n_tgt // 2
    my_tgt, my_src = lax.axis_index("tgt"), lax.axis_index("src")
    my_chip, my_core = my_tgt // 2, lax.rem(my_tgt, 2)
    sibling = my_chip * 2 + 1 - my_core
    my_group, my_place = my_src // owners, lax.rem(my_src, owners)

    def target_at(k):
        return lax.rem(my_group + 1 + k // per_step, steps) * per_step + lax.rem(k, per_step)

    def coupling_copy(k):
        return pltpu.make_async_copy(coup_ref.at[target_at(k)], held.at[k], held_sem.at[k])

    def same_core(hop):
        return lax.rem(my_chip + hop, chips) * 2 + my_core

    barrier = pltpu.get_barrier_semaphore()
    pl.semaphore_signal(barrier, inc=1, device_id={"tgt": sibling}, device_id_type=MESH)
    for hop in range(1, chips):
        pl.semaphore_signal(barrier, inc=1, device_id={"tgt": same_core(hop)}, device_id_type=MESH)
    for hop in range(1, n_src):
        pl.semaphore_signal(barrier, inc=1, device_id={"src": lax.rem(my_src + hop, n_src)}, device_id_type=MESH)

    own = pl.ds(my_tgt * clusters, clusters)
    own_copy = pltpu.make_async_copy(mult_ref, gathered.at[own], own_sem)
    own_copy.start()
    for k in range(min(DEPTH, targets)):
        coupling_copy(k).start()
    pl.semaphore_wait(barrier, chips + n_src - 1)

    across = []
    for hop in range(1, chips):
        copy = pltpu.make_async_remote_copy(
            src_ref=mult_ref, dst_ref=gathered.at[own], send_sem=gather_send.at[hop], recv_sem=gather_recv.at[hop],
            device_id={"tgt": same_core(hop)}, device_id_type=MESH)
        copy.start()
        across.append(copy)
    passed = [pltpu.make_async_remote_copy(
        src_ref=mult_ref, dst_ref=gathered.at[own], send_sem=pass_send.at[0], recv_sem=pass_recv.at[0],
        device_id={"tgt": sibling}, device_id_type=MESH)]
    passed[0].start()

    def fill(tgt):
        high, low = split(gathered[pl.ds(tgt * clusters, clusters)])
        at = pl.ds(tgt * clusters + 1, clusters)
        panels[at, :nrhs] = high
        panels[at, nrhs:] = low

    panels[0] = jnp.zeros((2 * nrhs, rank), jnp.bfloat16)
    own_copy.wait()
    fill(my_tgt)
    passed[0].wait_recv()
    fill(sibling)
    for hop in range(1, chips):
        across[hop - 1].wait_recv()
        origin = lax.rem(my_chip + chips - hop, chips) * 2 + my_core
        at = gathered.at[pl.ds(origin * clusters, clusters)]
        copy = pltpu.make_async_remote_copy(
            src_ref=at, dst_ref=at, send_sem=pass_send.at[hop], recv_sem=pass_recv.at[hop],
            device_id={"tgt": sibling}, device_id_type=MESH)
        copy.start()
        passed.append(copy)
        fill(origin)
    for hop in range(1, chips):
        passed[hop].wait_recv()
        fill(lax.rem(my_chip + chips - hop, chips) * 2 + 1 - my_core)

    before = my_src * block - 1

    def part_copy(dest):
        return pltpu.make_async_remote_copy(
            src_ref=partial.at[pl.ds(pl.multiple_of(dest * rows, 8), rows)], dst_ref=received.at[my_src],
            send_sem=part_send.at[dest], recv_sem=part_recv.at[my_src],
            device_id={"src": dest}, device_id_type=MESH)

    def one_target(k, carry):
        @pl.when(k + DEPTH < targets)
        def _():
            coupling_copy(k + DEPTH).start()

        target = target_at(k)
        coupling_copy(k).wait()
        total = jnp.zeros((2 * nrhs, 2 * rank), jnp.float32)
        for first in range(0, slots, 2):
            pair = range(first, min(first + 2, slots))
            chosen = []
            for s in pair:
                chosen.append(panels[jnp.maximum(slot_ref[target, s] - before, 0)])
            left = jnp.concatenate(chosen, axis=1)
            high, low = split(held[k, first:first + len(pair)].reshape(len(pair) * rank, rank))
            right = jnp.concatenate([high, low], axis=1)
            total = total + jnp.dot(left, right, preferred_element_type=jnp.float32)
        total = total[:nrhs] + total[nrhs:]
        partial[pl.ds(pl.multiple_of(target * nrhs, 8), nrhs)] = total[:, :rank] + total[:, rank:]

        step = k // per_step
        group = lax.rem(my_group + 1 + step, steps)

        @pl.when(jnp.logical_and(lax.rem(k, per_step) == per_step - 1, step < steps - 1))
        def _():
            for o in range(owners):
                part_copy(group * owners + o).start()

        return carry

    lax.fori_loop(0, targets, one_target, 0)
    for o in range(1, owners):
        part_copy(my_group * owners + lax.rem(my_place + o, owners)).start()

    result = partial[pl.ds(pl.multiple_of(my_src * rows, 8), rows)]
    for hop in range(1, n_src):
        origin = lax.rem(my_src + hop, n_src)
        pltpu.make_async_remote_copy(
            src_ref=received.at[origin], dst_ref=received.at[origin], send_sem=part_send.at[origin],
            recv_sem=part_recv.at[origin], device_id={"src": origin}, device_id_type=MESH).wait_recv()
        result = result + received[origin]
    out_ref[...] = result

    for copy in across + passed:
        copy.wait_send()
    for hop in range(1, n_src):
        part_copy(lax.rem(my_src + hop, n_src)).wait_send()


def body(n_tgt, n_src, multipoles, couplings, slot_sources):
    clusters, nrhs, rank = multipoles.shape
    targets, slots = couplings.shape[:2]
    rows = targets * nrhs // n_src
    chips = n_tgt // 2
    dma = pltpu.SemaphoreType.DMA
    return pl.pallas_call(
        functools.partial(kernel, n_tgt, n_src),
        out_shape=jax.ShapeDtypeStruct((rows, rank), jnp.float32),
        in_specs=[
            pl.BlockSpec(memory_space=pl.ANY),
            pl.BlockSpec(memory_space=pl.ANY),
            pl.BlockSpec(memory_space=pltpu.SMEM),
        ],
        out_specs=pl.BlockSpec(memory_space=pltpu.VMEM),
        scratch_shapes=[
            pltpu.VMEM((targets, slots, rank, rank), jnp.float32),
            pltpu.VMEM((n_tgt * clusters, nrhs, rank), jnp.float32),
            pltpu.VMEM((n_tgt * clusters + 1, 2 * nrhs, rank), jnp.bfloat16),
            pltpu.VMEM((targets * nrhs, rank), jnp.float32),
            pltpu.VMEM((n_src, rows, rank), jnp.float32),
            dma((targets,)),
            dma,
            dma((chips,)),
            dma((chips,)),
            dma((chips,)),
            dma((chips,)),
            dma((n_src,)),
            dma((n_src,)),
        ],
        compiler_params=pltpu.CompilerParams(
            collective_id=0, has_side_effects=True, vmem_limit_bytes=48 * 1024 * 1024),
        cost_estimate=pl.CostEstimate(
            flops=2 * targets * slots * nrhs * rank * rank, bytes_accessed=4 * targets * slots * rank * rank,
            transcendentals=0),
    )(multipoles, couplings, slot_sources)


def solution(mesh):
    placed = (P(("src", "tgt"), None, None), P("tgt", "src", None, None), P("tgt", "src"))
    return jax.shard_map(
        functools.partial(body, mesh.shape["tgt"], mesh.shape["src"]), mesh=mesh, in_specs=placed,
        out_specs=P(("tgt", "src"), None), check_vma=False
    )
```

```python
import functools

import jax
import jax.numpy as jnp
from jax import lax
from jax.experimental import pallas as pl
from jax.experimental.pallas import tpu as pltpu
from jax.sharding import PartitionSpec as P

MESH = pl.DeviceIdType.MESH
DEPTH = 8
UNROLL = 2
PARTS = 1


def split(value):
    high = value.astype(jnp.bfloat16)
    low = (value - high.astype(jnp.float32)).astype(jnp.bfloat16)
    return high, low


def kernel(n_tgt, n_src, mult_ref, coup_ref, list_ref, out_ref, slot_ref, held, gathered, panels, partial, received,
           list_sem, held_sem, own_sem, gather_send, gather_recv, pass_send, pass_recv, part_send, part_recv):
    targets, slots, rank = held.shape[:3]
    clusters, nrhs = mult_ref.shape[:2]
    block = n_tgt * clusters
    rows = out_ref.shape[0]
    steps = min(n_src, targets)
    per_step = targets // steps
    owners = n_src // steps
    chips = n_tgt // 2
    my_tgt, my_src = lax.axis_index("tgt"), lax.axis_index("src")
    my_chip, my_core = my_tgt // 2, lax.rem(my_tgt, 2)
    sibling = my_chip * 2 + 1 - my_core
    my_group, my_place = my_src // owners, lax.rem(my_src, owners)

    def target_at(k):
        return lax.rem(my_group + 1 + k // per_step, steps) * per_step + lax.rem(k, per_step)

    def coupling_copy(k):
        return pltpu.make_async_copy(coup_ref.at[target_at(k)], held.at[k], held_sem.at[k])

    def same_core(hop):
        return lax.rem(my_chip + hop, chips) * 2 + my_core

    barrier = pltpu.get_barrier_semaphore()
    pl.semaphore_signal(barrier, inc=1, device_id={"tgt": sibling}, device_id_type=MESH)
    for hop in range(1, chips):
        pl.semaphore_signal(barrier, inc=1, device_id={"tgt": same_core(hop)}, device_id_type=MESH)
    for hop in range(1, n_src):
        pl.semaphore_signal(barrier, inc=1, device_id={"src": lax.rem(my_src + hop, n_src)}, device_id_type=MESH)

    own = pl.ds(my_tgt * clusters, clusters)
    own_copy = pltpu.make_async_copy(mult_ref, gathered.at[own], own_sem)
    own_copy.start()
    list_copy = pltpu.make_async_copy(list_ref, slot_ref, list_sem)
    list_copy.start()
    for k in range(min(DEPTH, targets)):
        coupling_copy(k).start()
    pl.semaphore_wait(barrier, chips + n_src - 1)

    part = clusters // PARTS

    def panel_copy(origin, piece, dest, send_sem, recv_sem, src_ref=None):
        at = pl.ds(origin * clusters + piece * part, part)
        return pltpu.make_async_remote_copy(
            src_ref=gathered.at[at] if src_ref is None else src_ref, dst_ref=gathered.at[at], send_sem=send_sem,
            recv_sem=recv_sem, device_id={"tgt": dest}, device_id_type=MESH)

    across, passed = [], []
    for piece in range(PARTS):
        for hop in range(1, chips):
            across.append(panel_copy(
                my_tgt, piece, same_core(hop), gather_send.at[hop, piece], gather_recv.at[hop, piece],
                mult_ref.at[pl.ds(piece * part, part)]))
            across[-1].start()
    passed.append(pltpu.make_async_remote_copy(
        src_ref=mult_ref, dst_ref=gathered.at[own], send_sem=pass_send.at[0, 0], recv_sem=pass_recv.at[0, 0],
        device_id={"tgt": sibling}, device_id_type=MESH))
    passed[0].start()

    def fill(tgt, piece=0, count=clusters):
        at = tgt * clusters + piece * count
        high, low = split(gathered[pl.ds(at, count)])
        panels[pl.ds(at + 1, count), :nrhs] = high
        panels[pl.ds(at + 1, count), nrhs:] = low

    panels[0] = jnp.zeros((2 * nrhs, rank), jnp.bfloat16)
    list_copy.wait()
    own_copy.wait()
    fill(my_tgt)
    passed[0].wait_recv()
    fill(sibling)
    pieces = [(piece, hop) for piece in range(PARTS) for hop in range(1, chips)]
    for number, (piece, hop) in enumerate(pieces):
        across[number].wait_recv()
        origin = lax.rem(my_chip + chips - hop, chips) * 2 + my_core
        passed.append(panel_copy(origin, piece, sibling, pass_send.at[hop, piece], pass_recv.at[hop, piece]))
        passed[-1].start()
        fill(origin, piece, part)
    for number, (piece, hop) in enumerate(pieces):
        passed[number + 1].wait_recv()
        fill(lax.rem(my_chip + chips - hop, chips) * 2 + 1 - my_core, piece, part)

    before = my_src * block - 1

    def part_copy(dest):
        return pltpu.make_async_remote_copy(
            src_ref=partial.at[pl.ds(pl.multiple_of(dest * rows, 8), rows)], dst_ref=received.at[my_src],
            send_sem=part_send.at[dest], recv_sem=part_recv.at[my_src],
            device_id={"src": dest}, device_id_type=MESH)

    def one_target(target, couplings):
        total = jnp.zeros((2 * nrhs, 2 * rank), jnp.float32)
        for s in range(slots):
            left = panels[jnp.maximum(slot_ref[target, s] - before, 0)]
            right = jnp.concatenate(split(couplings[s]), axis=1)
            total = total + jnp.dot(left, right, preferred_element_type=jnp.float32)
        total = total[:nrhs] + total[nrhs:]
        partial[pl.ds(pl.multiple_of(target * nrhs, 8), nrhs)] = total[:, :rank] + total[:, rank:]

    def one_turn(turn, carry):
        for k in range(UNROLL):
            k = turn * UNROLL + k

            @pl.when(k + DEPTH < targets)
            def _():
                coupling_copy(k + DEPTH).start()

        for k in range(UNROLL):
            coupling_copy(turn * UNROLL + k).wait()
        for k in range(UNROLL):
            k = turn * UNROLL + k
            one_target(target_at(k), held.at[k])
        for k in range(UNROLL):
            k = turn * UNROLL + k
            step = k // per_step
            group = lax.rem(my_group + 1 + step, steps)

            @pl.when(jnp.logical_and(lax.rem(k, per_step) == per_step - 1, step < steps - 1))
            def _():
                for o in range(owners):
                    part_copy(group * owners + o).start()

        return carry

    lax.fori_loop(0, targets // UNROLL, one_turn, 0)
    for o in range(1, owners):
        part_copy(my_group * owners + lax.rem(my_place + o, owners)).start()

    result = partial[pl.ds(pl.multiple_of(my_src * rows, 8), rows)]
    for hop in range(1, n_src):
        origin = lax.rem(my_src + hop, n_src)
        pltpu.make_async_remote_copy(
            src_ref=received.at[origin], dst_ref=received.at[origin], send_sem=part_send.at[origin],
            recv_sem=part_recv.at[origin], device_id={"src": origin}, device_id_type=MESH).wait_recv()
        result = result + received[origin]
    out_ref[...] = result

    for copy in across + passed:
        copy.wait_send()
    for hop in range(1, n_src):
        part_copy(lax.rem(my_src + hop, n_src)).wait_send()


def body(n_tgt, n_src, multipoles, couplings, slot_sources):
    clusters, nrhs, rank = multipoles.shape
    targets, slots = couplings.shape[:2]
    rows = targets * nrhs // n_src
    chips = n_tgt // 2
    dma = pltpu.SemaphoreType.DMA
    return pl.pallas_call(
        functools.partial(kernel, n_tgt, n_src),
        out_shape=jax.ShapeDtypeStruct((rows, rank), jnp.float32),
        in_specs=[
            pl.BlockSpec(memory_space=pltpu.HBM),
            pl.BlockSpec(memory_space=pltpu.HBM),
            pl.BlockSpec(memory_space=pltpu.HBM),
        ],
        out_specs=pl.BlockSpec(memory_space=pltpu.VMEM),
        scratch_shapes=[
            pltpu.SMEM((targets, slots), jnp.int32),
            pltpu.VMEM((targets, slots, rank, rank), jnp.float32),
            pltpu.VMEM((n_tgt * clusters, nrhs, rank), jnp.float32),
            pltpu.VMEM((n_tgt * clusters + 1, 2 * nrhs, rank), jnp.bfloat16),
            pltpu.VMEM((targets * nrhs, rank), jnp.float32),
            pltpu.VMEM((n_src, rows, rank), jnp.float32),
            dma,
            dma((targets,)),
            dma,
            dma((chips, PARTS)),
            dma((chips, PARTS)),
            dma((chips, PARTS)),
            dma((chips, PARTS)),
            dma((n_src,)),
            dma((n_src,)),
        ],
        compiler_params=pltpu.CompilerParams(
            collective_id=0, has_side_effects=True, vmem_limit_bytes=48 * 1024 * 1024),
        cost_estimate=pl.CostEstimate(
            flops=2 * targets * slots * nrhs * rank * rank, bytes_accessed=4 * targets * slots * rank * rank,
            transcendentals=0),
    )(multipoles, couplings, slot_sources)


def solution(mesh):
    placed = (P(("src", "tgt"), None, None), P("tgt", "src", None, None), P("tgt", "src"))
    return jax.shard_map(
        functools.partial(body, mesh.shape["tgt"], mesh.shape["src"]), mesh=mesh, in_specs=placed,
        out_specs=P(("tgt", "src"), None), check_vma=False
    )
```

```python
import functools

import jax
import jax.numpy as jnp
from jax import lax
from jax.experimental import pallas as pl
from jax.experimental.pallas import tpu as pltpu
from jax.sharding import PartitionSpec as P

MESH = pl.DeviceIdType.MESH
DEPTH = 12
UNROLL = 4
PARTS = 1


def split(value):
    high = value.astype(jnp.bfloat16)
    low = (value - high.astype(jnp.float32)).astype(jnp.bfloat16)
    return high, low


def kernel(n_tgt, n_src, mult_ref, coup_ref, list_ref, out_ref, slot_ref, held, gathered, panels, partial, received,
           list_sem, held_sem, own_sem, gather_send, gather_recv, pass_send, pass_recv, part_send, part_recv):
    targets, slots, rank = held.shape[:3]
    clusters, nrhs = mult_ref.shape[:2]
    block = n_tgt * clusters
    rows = out_ref.shape[0]
    steps = min(n_src, targets)
    per_step = targets // steps
    owners = n_src // steps
    chips = n_tgt // 2
    my_tgt, my_src = lax.axis_index("tgt"), lax.axis_index("src")
    my_chip, my_core = my_tgt // 2, lax.rem(my_tgt, 2)
    sibling = my_chip * 2 + 1 - my_core
    my_group, my_place = my_src // owners, lax.rem(my_src, owners)

    def target_at(k):
        return lax.rem(my_group + 1 + k // per_step, steps) * per_step + lax.rem(k, per_step)

    def coupling_copy(k):
        return pltpu.make_async_copy(coup_ref.at[target_at(k)], held.at[k], held_sem.at[k])

    def same_core(hop):
        return lax.rem(my_chip + hop, chips) * 2 + my_core

    barrier = pltpu.get_barrier_semaphore()
    pl.semaphore_signal(barrier, inc=1, device_id={"tgt": sibling}, device_id_type=MESH)
    for hop in range(1, chips):
        pl.semaphore_signal(barrier, inc=1, device_id={"tgt": same_core(hop)}, device_id_type=MESH)
    for hop in range(1, n_src):
        pl.semaphore_signal(barrier, inc=1, device_id={"src": lax.rem(my_src + hop, n_src)}, device_id_type=MESH)

    own = pl.ds(my_tgt * clusters, clusters)
    own_copy = pltpu.make_async_copy(mult_ref, gathered.at[own], own_sem)
    own_copy.start()
    list_copy = pltpu.make_async_copy(list_ref, slot_ref, list_sem)
    list_copy.start()
    for k in range(min(DEPTH, targets)):
        coupling_copy(k).start()
    pl.semaphore_wait(barrier, chips + n_src - 1)

    part = clusters // PARTS

    def panel_copy(origin, piece, dest, send_sem, recv_sem, src_ref=None):
        at = pl.ds(origin * clusters + piece * part, part)
        return pltpu.make_async_remote_copy(
            src_ref=gathered.at[at] if src_ref is None else src_ref, dst_ref=gathered.at[at], send_sem=send_sem,
            recv_sem=recv_sem, device_id={"tgt": dest}, device_id_type=MESH)

    across, passed = [], []
    for piece in range(PARTS):
        for hop in range(1, chips):
            across.append(panel_copy(
                my_tgt, piece, same_core(hop), gather_send.at[hop, piece], gather_recv.at[hop, piece],
                mult_ref.at[pl.ds(piece * part, part)]))
            across[-1].start()
    passed.append(pltpu.make_async_remote_copy(
        src_ref=mult_ref, dst_ref=gathered.at[own], send_sem=pass_send.at[0, 0], recv_sem=pass_recv.at[0, 0],
        device_id={"tgt": sibling}, device_id_type=MESH))
    passed[0].start()

    def fill(tgt, piece=0, count=clusters):
        at = tgt * clusters + piece * count
        high, low = split(gathered[pl.ds(at, count)])
        panels[pl.ds(at + 1, count), :nrhs] = high
        panels[pl.ds(at + 1, count), nrhs:] = low

    panels[0] = jnp.zeros((2 * nrhs, rank), jnp.bfloat16)
    list_copy.wait()
    own_copy.wait()
    fill(my_tgt)
    passed[0].wait_recv()
    fill(sibling)
    pieces = [(piece, hop) for piece in range(PARTS) for hop in range(1, chips)]
    for number, (piece, hop) in enumerate(pieces):
        across[number].wait_recv()
        origin = lax.rem(my_chip + chips - hop, chips) * 2 + my_core
        passed.append(panel_copy(origin, piece, sibling, pass_send.at[hop, piece], pass_recv.at[hop, piece]))
        passed[-1].start()
        fill(origin, piece, part)
    for number, (piece, hop) in enumerate(pieces):
        passed[number + 1].wait_recv()
        fill(lax.rem(my_chip + chips - hop, chips) * 2 + 1 - my_core, piece, part)

    before = my_src * block - 1

    def part_copy(dest):
        return pltpu.make_async_remote_copy(
            src_ref=partial.at[pl.ds(pl.multiple_of(dest * rows, 8), rows)], dst_ref=received.at[my_src],
            send_sem=part_send.at[dest], recv_sem=part_recv.at[my_src],
            device_id={"src": dest}, device_id_type=MESH)

    def one_target(target, couplings):
        total = jnp.zeros((2 * nrhs, 2 * rank), jnp.float32)
        for s in range(slots):
            left = panels[jnp.maximum(slot_ref[target, s] - before, 0)]
            right = jnp.concatenate(split(couplings[s]), axis=1)
            total = total + jnp.dot(left, right, preferred_element_type=jnp.float32)
        total = total[:nrhs] + total[nrhs:]
        partial[pl.ds(pl.multiple_of(target * nrhs, 8), nrhs)] = total[:, :rank] + total[:, rank:]

    def one_turn(turn, carry):
        for k in range(UNROLL):
            k = turn * UNROLL + k

            @pl.when(k + DEPTH < targets)
            def _():
                coupling_copy(k + DEPTH).start()

        for k in range(UNROLL):
            coupling_copy(turn * UNROLL + k).wait()
        for k in range(UNROLL):
            k = turn * UNROLL + k
            one_target(target_at(k), held.at[k])
        for k in range(UNROLL):
            k = turn * UNROLL + k
            step = k // per_step
            group = lax.rem(my_group + 1 + step, steps)

            @pl.when(jnp.logical_and(lax.rem(k, per_step) == per_step - 1, step < steps - 1))
            def _():
                for o in range(owners):
                    part_copy(group * owners + o).start()

        return carry

    lax.fori_loop(0, targets // UNROLL, one_turn, 0)
    for o in range(1, owners):
        part_copy(my_group * owners + lax.rem(my_place + o, owners)).start()

    result = partial[pl.ds(pl.multiple_of(my_src * rows, 8), rows)]
    for hop in range(1, n_src):
        origin = lax.rem(my_src + hop, n_src)
        pltpu.make_async_remote_copy(
            src_ref=received.at[origin], dst_ref=received.at[origin], send_sem=part_send.at[origin],
            recv_sem=part_recv.at[origin], device_id={"src": origin}, device_id_type=MESH).wait_recv()
        result = result + received[origin]
    out_ref[...] = result

    for copy in across + passed:
        copy.wait_send()
    for hop in range(1, n_src):
        part_copy(lax.rem(my_src + hop, n_src)).wait_send()


def body(n_tgt, n_src, multipoles, couplings, slot_sources):
    clusters, nrhs, rank = multipoles.shape
    targets, slots = couplings.shape[:2]
    rows = targets * nrhs // n_src
    chips = n_tgt // 2
    dma = pltpu.SemaphoreType.DMA
    return pl.pallas_call(
        functools.partial(kernel, n_tgt, n_src),
        out_shape=jax.ShapeDtypeStruct((rows, rank), jnp.float32),
        in_specs=[
            pl.BlockSpec(memory_space=pltpu.HBM),
            pl.BlockSpec(memory_space=pltpu.HBM),
            pl.BlockSpec(memory_space=pltpu.HBM),
        ],
        out_specs=pl.BlockSpec(memory_space=pltpu.VMEM),
        scratch_shapes=[
            pltpu.SMEM((targets, slots), jnp.int32),
            pltpu.VMEM((targets, slots, rank, rank), jnp.float32),
            pltpu.VMEM((n_tgt * clusters, nrhs, rank), jnp.float32),
            pltpu.VMEM((n_tgt * clusters + 1, 2 * nrhs, rank), jnp.bfloat16),
            pltpu.VMEM((targets * nrhs, rank), jnp.float32),
            pltpu.VMEM((n_src, rows, rank), jnp.float32),
            dma,
            dma((targets,)),
            dma,
            dma((chips, PARTS)),
            dma((chips, PARTS)),
            dma((chips, PARTS)),
            dma((chips, PARTS)),
            dma((n_src,)),
            dma((n_src,)),
        ],
        compiler_params=pltpu.CompilerParams(
            collective_id=0, has_side_effects=True, vmem_limit_bytes=48 * 1024 * 1024),
        cost_estimate=pl.CostEstimate(
            flops=2 * targets * slots * nrhs * rank * rank, bytes_accessed=4 * targets * slots * rank * rank,
            transcendentals=0),
    )(multipoles, couplings, slot_sources)


def solution(mesh):
    placed = (P(("src", "tgt"), None, None), P("tgt", "src", None, None), P("tgt", "src"))
    return jax.shard_map(
        functools.partial(body, mesh.shape["tgt"], mesh.shape["src"]), mesh=mesh, in_specs=placed,
        out_specs=P(("tgt", "src"), None), check_vma=False
    )
```
